32 devices in a mesh: grp: 2 (over y), ctx: 4 (over z), head: 4 (over x, core).
Axes of the slice: x: 2, y: 2, z: 4, core: 2. Of those that a mesh axis runs over, the one named last changes fastest.
Arguments:
- queries: bfloat16 [16384, 2048], P(('grp', 'ctx', 'head')), parts along dimension 0, may hold values from -6 to 6
- keys: bfloat16 [16384, 2048], P(('grp', 'ctx', 'head')), parts along dimension 0, may hold values from -6 to 6
- values: bfloat16 [16384, 2048], P(('grp', 'ctx', 'head')), parts along dimension 0, may hold values from -6 to 6
- out_grad: bfloat16 [16384, 2048], P(('grp', 'ctx', 'head')), parts along dimension 0, may hold values from -6 to 6
- level_table: float32 [8, 21, 16], P(None, None, 'head'), may hold values from 0.25 to 2
- selector: int32 [256], P(('grp', 'ctx')), parts along dimension 0, may hold values from 0 to 7
Outputs:
- attn_out: bfloat16 [16384, 2048], P(('grp', 'ctx', 'head')), parts along dimension 0
- query_grad: bfloat16 [16384, 2048], P(('grp', 'ctx', 'head')), parts along dimension 0
- key_grad: bfloat16 [16384, 2048], P(('grp', 'ctx', 'head')), parts along dimension 0
- value_grad: bfloat16 [16384, 2048], P(('grp', 'ctx', 'head')), parts along dimension 0
The draws below stay inside these ranges and needn't reach their ends.
There are 2 independent parts, one for each index of `grp`. The reference program is written for one: setup_inputs(seed, part) draws one part's arguments, and reference() takes and returns one part's arrays. A program takes and returns all parts, laid end to end along the dimension named above; an argument that names none is the same for every part. Nothing has to cross between parts.
Inputs may be any that keep to these rules, and one draw needn't show every extreme that they name: `selector`: each stretch's row of the weight table.
All inputs are finite; a program needn't handle non-finite values.
Results may differ from the reference program's by a relative error of at most 0.0051.
Values may be sent and summed in bfloat16 or wider, within the bound.
A program may use at most 256 MiB of HBM per device.

```python
import math
import jax
import jax.numpy as jnp
import numpy as np
from jax import lax

H = 16
DK = 128
STRETCH = 64
LEVELS = 21
SEL = 8
TOK_DEV = 2048
TOKENS = 8192
STRETCHES = 128
CTX_BITS = 2
N_CTX = 4


def plant(result, key, smallest, top_value):
    longest = result.shape.index(max(result.shape))
    spots = []
    for shift in (0, 1):
        where = [jax.random.randint(jax.random.fold_in(key, axis), (), 0, length) for axis, length in enumerate(result.shape)]
        where[longest] = (where[longest] + shift) % result.shape[longest]
        spots.append(tuple(where))
    return result.at[spots[0]].set(smallest).at[spots[1]].set(top_value)


def levels(rng, dims, pieces, low, top_value):
    def one(dim, shards_of):
        steps = jax.random.uniform(jax.random.fold_in(jax.random.fold_in(rng, 6), dim), (shards_of,), jnp.float32, low / len(pieces), top_value / len(pieces))
        return jnp.repeat(jnp.exp(steps), dims[dim] // shards_of).reshape((-1,) + (1,) * (len(dims) - dim - 1))

    loudness = one(*pieces[0])
    for cut in pieces[1:]:
        loudness = loudness * one(*cut)
    return loudness


def normal_values(key, dims, spread, reach, pieces=(), kind=jnp.bfloat16):
    result = spread * jax.random.normal(key, dims, jnp.float32)
    if pieces:
        result = result * levels(key, dims, pieces, -0.22, 0.18)
    return jnp.clip(result, -reach, reach).astype(kind)


def setup_inputs(seed: int = 0, part: int = 0) -> dict:
    arg_keys = jax.random.split(jax.random.key(seed), 7)
    part_keys = jax.random.split(jax.random.fold_in(arg_keys[6], part), 7)
    return {
        "queries": normal_values(part_keys[0], (TOKENS, H * DK), 1.0, 6.0, ((0, 16),)),
        "keys": normal_values(part_keys[1], (TOKENS, H * DK), 1.0, 6.0, ((0, 16),)),
        "values": normal_values(part_keys[2], (TOKENS, H * DK), 1.0, 6.0, ((0, 16),)),
        "out_grad": normal_values(part_keys[3], (TOKENS, H * DK), 1.0, 6.0, ((0, 16),)),
        "level_table": jnp.clip(jnp.exp(math.log(2.0) - 2.0794415 * jax.random.uniform(arg_keys[4], (SEL, LEVELS, H), jnp.float32) ** levels(arg_keys[4], (SEL, LEVELS, H), ((2, 4),), -0.2, 0.2)), 0.25, 2.0),
        "selector": plant(jax.random.randint(part_keys[5], (STRETCHES,), 0, SEL), jax.random.fold_in(part_keys[5], 1), 0, SEL - 1).astype(jnp.int32),
    }


HIGHEST = lax.Precision.HIGHEST

def level_of(xor_value, limit):
    count = jnp.zeros(xor_value.shape, jnp.int32)
    power = 1
    while power < limit:
        count = count + (xor_value >= power).astype(jnp.int32)
        power = power * 2
    return count

def scaled_table(level_table, selector):
    level_ids = jnp.arange(LEVELS, dtype=jnp.int32).astype(jnp.float32)
    scaling = jnp.exp2(-0.5 * jnp.maximum(level_ids - 1.0, 0.0)) / math.sqrt(DK)
    return level_table[selector] * scaling[None, :, None]

def rounded(array_in):
    return lax.optimization_barrier(array_in.astype(jnp.bfloat16)).astype(jnp.float32)

def block_masks():
    forward = np.zeros((N_CTX, CTX_BITS, N_CTX), np.float32)
    backward = np.zeros((N_CTX, CTX_BITS, N_CTX), np.float32)
    for block_index in range(N_CTX):
        for bit_index in range(CTX_BITS):
            low_start = block_index >> bit_index + 1 << bit_index + 1
            span_size = 1 << bit_index
            upper_bit = block_index >> bit_index & 1
            forward[block_index, bit_index, low_start:low_start + span_size] = upper_bit
            backward[block_index, bit_index, low_start + span_size:low_start + 2 * span_size] = 1 - upper_bit
    return (forward, backward)

def reference(queries, keys, values, out_grad, level_table, selector):
    head_shape = (N_CTX, TOK_DEV, H, DK)
    query_blocks = queries.reshape(head_shape)
    key_blocks = keys.reshape(head_shape)
    value_blocks = values.reshape(head_shape)
    grad_blocks = out_grad.reshape(head_shape)
    per_stretch = scaled_table(level_table, selector)
    stretch_blocks = per_stretch.reshape(N_CTX, TOK_DEV // STRETCH, LEVELS, H)
    lower = TOK_DEV.bit_length() - 1
    cross_weights = stretch_blocks[:, :, lower + 1:lower + 1 + CTX_BITS, :]
    positions = jnp.arange(TOK_DEV, dtype=jnp.int32)
    level_index = level_of(jnp.bitwise_xor(positions[:, None], positions[None, :]), TOK_DEV).astype(jnp.int32)
    causal = positions[None, :] <= positions[:, None]

    def local_part(inputs):
        query_rows, key_rows, value_rows, grad_rows, stretch_weights, cross_part = inputs
        query_float = query_rows.astype(jnp.float32)
        key_float = key_rows.astype(jnp.float32)
        value_float = value_rows.astype(jnp.float32)
        grad_float = grad_rows.astype(jnp.float32)
        token_weights = jnp.repeat(jnp.transpose(stretch_weights, (2, 0, 1)), STRETCH, axis=1)
        weight = jnp.take_along_axis(token_weights, jnp.broadcast_to(level_index[None], (H, TOK_DEV, TOK_DEV)), axis=2)
        weight = jnp.where(causal[None], weight, 0.0)
        scores = jnp.einsum('thd,shd->hts', query_float, key_float, precision=HIGHEST)
        attn = rounded(scores * weight)
        out_local = jnp.einsum('hts,shd->thd', attn, value_float, precision=HIGHEST)
        grad_scores = jnp.einsum('thd,shd->hts', grad_float, value_float, precision=HIGHEST)
        score_grads = rounded(grad_scores * weight)
        query_local = jnp.einsum('hts,shd->thd', score_grads, key_float, precision=HIGHEST)
        key_local = jnp.einsum('hts,thd->shd', score_grads, query_float, precision=HIGHEST)
        value_local = jnp.einsum('hts,thd->shd', attn, grad_float, precision=HIGHEST)
        state = jnp.einsum('shd,she->hde', key_float, value_float, precision=HIGHEST)
        stretch_query = query_float.reshape(TOK_DEV // STRETCH, STRETCH, H, DK)
        stretch_grad = grad_float.reshape(TOK_DEV // STRETCH, STRETCH, H, DK)
        outer = jnp.einsum('cthd,cthe->chde', stretch_query, stretch_grad, precision=HIGHEST)
        adjoint = jnp.einsum('cjh,chde->jhde', cross_part, outer, precision=HIGHEST)
        return (out_local, query_local, key_local, value_local, state, adjoint)
    out_local, query_local, key_local, value_local, states, adjoints = lax.map(local_part, (query_blocks, key_blocks, value_blocks, grad_blocks, stretch_blocks, cross_weights))
    forward_mask, backward_mask = block_masks()
    level_stack = jnp.einsum('ijn,nhde->ijhde', jnp.asarray(forward_mask), states, precision=HIGHEST)
    returned = rounded(jnp.einsum('ijn,njhde->ihde', jnp.asarray(backward_mask), adjoints, precision=HIGHEST))

    def cross_part_fn(inputs):
        query_rows, key_rows, value_rows, grad_rows, cross_part, stack_here, back_here = inputs
        mixed = rounded(jnp.einsum('cjh,jhde->chde', cross_part, stack_here, precision=HIGHEST))
        stretch_query = query_rows.astype(jnp.float32).reshape(TOK_DEV // STRETCH, STRETCH, H, DK)
        stretch_grad = grad_rows.astype(jnp.float32).reshape(TOK_DEV // STRETCH, STRETCH, H, DK)
        out_cross = jnp.einsum('cthd,chde->cthe', stretch_query, mixed, precision=HIGHEST).reshape(TOK_DEV, H, DK)
        query_cross = jnp.einsum('cthe,chde->cthd', stretch_grad, mixed, precision=HIGHEST).reshape(TOK_DEV, H, DK)
        key_cross = jnp.einsum('she,hde->shd', value_rows.astype(jnp.float32), back_here, precision=HIGHEST)
        value_cross = jnp.einsum('shd,hde->she', key_rows.astype(jnp.float32), back_here, precision=HIGHEST)
        return (out_cross, query_cross, key_cross, value_cross)
    out_cross, query_cross, key_cross, value_cross = lax.map(cross_part_fn, (query_blocks, key_blocks, value_blocks, grad_blocks, cross_weights, level_stack, returned))
    flat_shape = (TOKENS, H * DK)
    attn_out = (out_local + out_cross).astype(jnp.bfloat16).reshape(flat_shape)
    query_grad = (query_local + query_cross).astype(jnp.bfloat16).reshape(flat_shape)
    key_grad = (key_local + key_cross).astype(jnp.bfloat16).reshape(flat_shape)
    value_grad = (value_local + value_cross).astype(jnp.bfloat16).reshape(flat_shape)
    return (attn_out, query_grad, key_grad, value_grad)
```

```python
import functools
import math

import jax
import jax.numpy as jnp
from jax import lax
from jax.experimental import pallas as pl
from jax.experimental.pallas import tpu as pltpu
from jax.sharding import PartitionSpec as P

F32 = jnp.float32
BF16 = jnp.bfloat16
STRETCH = 64
TILE = 128
NT = (((1,), (1,)), ((), ()))
TN = (((0,), (0,)), ((), ()))
NN = (((1,), (0,)), ((), ()))
VMEM_LIMIT = 40 * 1024 * 1024


def mm(a, b, dims):
    return lax.dot_general(a, b, dims, preferred_element_type=F32)


def state_kernel(bits, low, lam, q, k, v, g, out):
    head = pl.program_id(0)
    tok, width = q.shape
    out[0, 0] = mm(k[...], v[...], TN).astype(BF16)
    grad = g[...].astype(F32)
    cols = []
    for j in range(bits):
        rows = [
            grad[c * STRETCH : (c + 1) * STRETCH] * lam[head, c, low + 1 + j]
            for c in range(tok // STRETCH)
        ]
        cols.append(jnp.concatenate(rows, axis=0).astype(BF16))
    outer = mm(q[...], jnp.concatenate(cols, axis=1), TN)
    for j in range(bits):
        out[bits - j, 0] = outer[:, j * width : (j + 1) * width].astype(BF16)


def dense_kernel(lam, a, b, x, y, o1, o2, prob):
    head = pl.program_id(0)
    tok = a.shape[0]
    ri = lax.broadcasted_iota(jnp.int32, (TILE, TILE), 0)
    ci = lax.broadcasted_iota(jnp.int32, (TILE, TILE), 1)
    xor = jnp.bitwise_xor(ri, ci)
    level = jnp.zeros((TILE, TILE), jnp.int32)
    tile_levels = TILE.bit_length() - 1
    for p in range(tile_levels):
        level = level + (xor >= (1 << p)).astype(jnp.int32)
    level = jnp.where(ci <= ri, level, -1)
    big = min(256, tok)
    for r0 in range(0, tok, big):
        cols = r0 + big
        scores = mm(a[r0 : r0 + big, :], b[:cols, :], NT)
        for r in range(r0 // TILE, (r0 + big) // TILE):
            for half in range(TILE // STRETCH):
                row = r * TILE + half * STRETCH
                c = row // STRETCH
                for t in range(cols // TILE):
                    part = scores[row - r0 : row - r0 + STRETCH, t * TILE : (t + 1) * TILE]
                    if t < r:
                        part = part * lam[head, c, tile_levels + (r ^ t).bit_length()]
                    elif t == r:
                        lev = level[half * STRETCH : (half + 1) * STRETCH]
                        weight = jnp.zeros((STRETCH, TILE), F32)
                        for i in range(tile_levels + 1):
                            weight = jnp.where(lev == i, lam[head, c, i], weight)
                        part = part * weight
                    else:
                        part = jnp.zeros_like(part)
                    prob[row : row + STRETCH, t * TILE : (t + 1) * TILE] = part.astype(BF16)
        o1[r0 : r0 + big, :] = mm(prob[r0 : r0 + big, :cols], x[:cols, :], NN).astype(BF16)
    for c0 in range(0, tok, big):
        o2[c0 : c0 + big, :] = mm(prob[c0:, c0 : c0 + big], y[c0:, :], TN).astype(BF16)


def cross_kernel(bits, lam, q, k, v, g, o_in, dq_in, dk_in, dv_in, x0, rest, r0, o, dq, dk, dv):
    head = pl.program_id(0)
    tok, width = q.shape
    back = (rest[bits - 1, 0].astype(F32) + r0[0].astype(F32)).astype(BF16)
    dk[...] = (dk_in[...].astype(F32) + mm(v[...], back, NT)).astype(BF16)
    dv[...] = (dv_in[...].astype(F32) + mm(k[...], back, NN)).astype(BF16)
    states = [x0[0]] + [rest[j, 0] for j in range(bits - 1)]
    fwd = mm(q[...], jnp.concatenate(states, axis=1), NN)
    bwd = mm(g[...], jnp.concatenate(states, axis=0), NT)
    for c in range(tok // STRETCH):
        rows = slice(c * STRETCH, (c + 1) * STRETCH)
        o_sum = o_in[rows, :].astype(F32)
        q_sum = dq_in[rows, :].astype(F32)
        for j in range(bits):
            scale = lam[head, c, j]
            o_sum = o_sum + fwd[rows, j * width : (j + 1) * width] * scale
            q_sum = q_sum + bwd[rows, j * width : (j + 1) * width] * scale
        o[rows, :] = o_sum.astype(BF16)
        dq[rows, :] = q_sum.astype(BF16)


def shards(queries, keys, values, out_grad, level_table, selector):
    head_n, ctx_n = lax.axis_size("head"), lax.axis_size("ctx")
    head_i, ctx_i = lax.axis_index("head"), lax.axis_index("ctx")
    head_bits, ctx_bits = head_n.bit_length() - 1, ctx_n.bit_length() - 1
    bits = head_bits + ctx_bits
    me = ctx_i * head_n + head_i
    tok = queries.shape[0]
    heads = level_table.shape[2] * head_n
    width = queries.shape[1] // heads
    low = tok.bit_length() - 1
    stretches = tok // STRETCH

    table = lax.all_gather(level_table, "head", axis=2, tiled=True)
    mine = lax.dynamic_slice(selector, (head_i * stretches,), (stretches,))
    ids = jnp.arange(level_table.shape[0], dtype=jnp.int32)
    hot = (mine[:, None] == ids[None, :]).astype(F32)
    lev = jnp.arange(level_table.shape[1], dtype=jnp.int32).astype(F32)
    scaling = jnp.exp2(-0.5 * jnp.maximum(lev - 1.0, 0.0)) / math.sqrt(width)
    picked = jnp.sum(hot[:, :, None, None] * table[None], axis=1)
    lam = jnp.transpose(picked * scaling[None, :, None], (2, 0, 1))
    bit_ids = jnp.arange(bits, dtype=jnp.int32)
    upper = (me >> bit_ids & 1).astype(F32)
    lam_cross = lam[:, :, low + 1 : low + 1 + bits] * upper[None, None, :]

    row_spec = pl.BlockSpec((tok, width), lambda h: (0, h))
    smem = pl.BlockSpec(memory_space=pltpu.SMEM)
    row_shape = jax.ShapeDtypeStruct(queries.shape, BF16)
    params = pltpu.CompilerParams(vmem_limit_bytes=VMEM_LIMIT)
    n_bytes = tok * heads * width * 2

    packet = pl.pallas_call(
        functools.partial(state_kernel, bits, low),
        grid=(heads,),
        in_specs=[smem] + [row_spec] * 4,
        out_specs=pl.BlockSpec((bits + 1, 1, width, width), lambda h: (0, h, 0, 0)),
        out_shape=jax.ShapeDtypeStruct((bits + 1, heads, width, width), BF16),
        compiler_params=params,
        name="states",
    )(lam, queries, keys, values, out_grad)

    def dense(a, b, x, y, name):
        return pl.pallas_call(
            dense_kernel,
            grid=(heads,),
            in_specs=[smem] + [row_spec] * 4,
            out_specs=[row_spec] * 2,
            out_shape=[row_shape] * 2,
            scratch_shapes=[pltpu.VMEM((tok, tok), BF16)],
            compiler_params=params,
            cost_estimate=pl.CostEstimate(
                flops=8 * heads * tok * tok * width, bytes_accessed=6 * n_bytes, transcendentals=0
            ),
            name=name,
        )(lam, a, b, x, y)

    o_part, dv_part = dense(queries, keys, values, out_grad, "dense_out")
    dq_part, dk_part = dense(out_grad, values, keys, queries, "dense_grad")

    def swap(array, bit):
        if bit < head_bits:
            pairs = [(i, i ^ (1 << bit)) for i in range(head_n)]
            return lax.ppermute(array, "head", pairs)
        step = 1 << (bit - head_bits)
        return lax.ppermute(array, "ctx", [(i, i ^ step) for i in range(ctx_n)])

    def bit_of(bit):
        return (me >> bit & 1) == 1

    half = heads // 2
    core = head_i & 1
    got_full = swap(jnp.where(bit_of(0), packet[bits], packet[0]), 0)
    state0 = got_full
    back0 = jnp.where(bit_of(0), jnp.zeros_like(got_full), got_full)
    keep_i, send_i = core * half, (1 - core) * half
    sent = lax.dynamic_slice_in_dim(packet[:bits], send_i, half, axis=1)
    kept = lax.dynamic_slice_in_dim(packet[:bits], keep_i, half, axis=1)
    run = (kept.astype(F32) + swap(sent, 0).astype(F32)).astype(BF16)
    states = []
    back = jnp.zeros((half, width, width), F32)
    for bit in range(1, bits):
        if bit < bits - 1:
            got = swap(run, bit)
            states.append(got[0])
            back = back + jnp.where(bit_of(bit), 0.0, got[-1].astype(F32))
            run = (run[:-1].astype(F32) + got[:-1].astype(F32)).astype(BF16)
        else:
            got = swap(jnp.where(bit_of(bit), run[1], run[0]), bit)
            states.append(got)
            back = back + jnp.where(bit_of(bit), 0.0, got.astype(F32))
    ours = jnp.stack(states + [back.astype(BF16)], axis=0)
    theirs = swap(ours, 0)
    rest = jnp.where(
        core == 0,
        jnp.concatenate([ours, theirs], axis=1),
        jnp.concatenate([theirs, ours], axis=1),
    )

    mat_spec = pl.BlockSpec((1, width, width), lambda h: (h, 0, 0))
    return pl.pallas_call(
        functools.partial(cross_kernel, bits),
        grid=(heads,),
        in_specs=[smem]
        + [row_spec] * 8
        + [mat_spec, pl.BlockSpec((bits, 1, width, width), lambda h: (0, h, 0, 0)), mat_spec],
        out_specs=[row_spec] * 4,
        out_shape=[row_shape] * 4,
        compiler_params=params,
        name="cross",
    )(
        lam_cross, queries, keys, values, out_grad,
        o_part, dq_part, dk_part, dv_part, state0, rest, back0,
    )


def solution(mesh):
    rows = P(("grp", "ctx", "head"), None)
    in_specs = (rows, rows, rows, rows, P(None, None, "head"), P(("grp", "ctx")))
    return jax.shard_map(
        shards, mesh=mesh, in_specs=in_specs, out_specs=(rows,) * 4, check_vma=False
    )
```

```python
import functools
import math

import jax
import jax.numpy as jnp
from jax import lax
from jax.experimental import pallas as pl
from jax.experimental.pallas import tpu as pltpu
from jax.sharding import PartitionSpec as P

F32 = jnp.float32
BF16 = jnp.bfloat16
STRETCH = 64
TILE = 128
NT = (((1,), (1,)), ((), ()))
TN = (((0,), (0,)), ((), ()))
NN = (((1,), (0,)), ((), ()))
VMEM_LIMIT = 62 * 1024 * 1024
GROUP = 2


def mm(a, b, dims):
    return lax.dot_general(a, b, dims, preferred_element_type=F32)


def state_kernel(bits, low, lam, q_all, k_all, v_all, g_all, out):
    tok = q_all.shape[0]
    width = q_all.shape[1] // GROUP
    for n in range(GROUP):
        head = pl.program_id(0) * GROUP + n
        lanes = slice(n * width, (n + 1) * width)
        q, k, v = q_all[:, lanes], k_all[:, lanes], v_all[:, lanes]
        grad = g_all[:, lanes].astype(F32)
        out[0, n] = mm(k, v, TN).astype(BF16)
        cols = []
        for j in range(bits):
            rows = [
                grad[c * STRETCH : (c + 1) * STRETCH] * lam[head, c, low + 1 + j]
                for c in range(tok // STRETCH)
            ]
            cols.append(jnp.concatenate(rows, axis=0).astype(BF16))
        outer = mm(q, jnp.concatenate(cols, axis=1), TN)
        for j in range(bits):
            out[bits - j, n] = outer[:, j * width : (j + 1) * width].astype(BF16)


def dense_kernel(lam, a, b, x, y, after, o1, o2, token, prob):
    del after
    tok = a.shape[0]
    width = a.shape[1] // GROUP
    token[...] = jnp.zeros_like(token)
    ri = lax.broadcasted_iota(jnp.int32, (TILE, TILE), 0)
    ci = lax.broadcasted_iota(jnp.int32, (TILE, TILE), 1)
    xor = jnp.bitwise_xor(ri, ci)
    level = jnp.zeros((TILE, TILE), jnp.int32)
    tile_levels = TILE.bit_length() - 1
    for p in range(tile_levels):
        level = level + (xor >= (1 << p)).astype(jnp.int32)
    level = jnp.where(ci <= ri, level, -1)
    big = min(256, tok)
    for n in range(GROUP):
        head = pl.program_id(0) * GROUP + n
        lanes = slice(n * width, (n + 1) * width)
        for r0 in range(0, tok, big):
            cols = r0 + big
            scores = mm(a[r0 : r0 + big, lanes], b[:cols, lanes], NT)
            for r in range(r0 // TILE, (r0 + big) // TILE):
                for half in range(TILE // STRETCH):
                    row = r * TILE + half * STRETCH
                    c = row // STRETCH
                    for t in range(cols // TILE):
                        part = scores[row - r0 : row - r0 + STRETCH, t * TILE : (t + 1) * TILE]
                        if t < r:
                            part = part * lam[head, c, tile_levels + (r ^ t).bit_length()]
                        elif t == r:
                            lev = level[half * STRETCH : (half + 1) * STRETCH]
                            weight = jnp.zeros((STRETCH, TILE), F32)
                            for i in range(tile_levels + 1):
                                weight = jnp.where(lev == i, lam[head, c, i], weight)
                            part = part * weight
                        else:
                            part = jnp.zeros_like(part)
                        prob[n, row : row + STRETCH, t * TILE : (t + 1) * TILE] = part.astype(BF16)
            o1[r0 : r0 + big, lanes] = mm(
                prob[n, r0 : r0 + big, :cols], x[:cols, lanes], NN
            ).astype(BF16)
        for c0 in range(0, tok, big):
            o2[c0 : c0 + big, lanes] = mm(
                prob[n, c0:, c0 : c0 + big], y[c0:, lanes], TN
            ).astype(BF16)


def cross_kernel(
    bits, lam, pick, q, k, v, g, o_in, dq_in, dk_in, dv_in, x0, ours, theirs, r0, o, dq, dk, dv
):
    tok = q.shape[0]
    width = q.shape[1] // GROUP
    own = pick[pl.program_id(0)] == 1
    for n in range(GROUP):
        head = pl.program_id(0) * GROUP + n
        lanes = slice(n * width, (n + 1) * width)
        rest = [jnp.where(own, ours[j, n], theirs[j, n]) for j in range(bits)]
        back = (rest[bits - 1].astype(F32) + r0[n].astype(F32)).astype(BF16)
        dk[:, lanes] = (dk_in[:, lanes].astype(F32) + mm(v[:, lanes], back, NT)).astype(BF16)
        dv[:, lanes] = (dv_in[:, lanes].astype(F32) + mm(k[:, lanes], back, NN)).astype(BF16)
        states = [x0[n]] + rest[: bits - 1]
        fwd = mm(q[:, lanes], jnp.concatenate(states, axis=1), NN)
        bwd = mm(g[:, lanes], jnp.concatenate(states, axis=0), NT)
        for c in range(tok // STRETCH):
            rows = slice(c * STRETCH, (c + 1) * STRETCH)
            o_sum = o_in[rows, lanes].astype(F32)
            q_sum = dq_in[rows, lanes].astype(F32)
            for j in range(bits):
                scale = lam[head, c, j]
                o_sum = o_sum + fwd[rows, j * width : (j + 1) * width] * scale
                q_sum = q_sum + bwd[rows, j * width : (j + 1) * width] * scale
            o[rows, lanes] = o_sum.astype(BF16)
            dq[rows, lanes] = q_sum.astype(BF16)


def shards(queries, keys, values, out_grad, level_table, selector):
    head_n, ctx_n = lax.axis_size("head"), lax.axis_size("ctx")
    head_i, ctx_i = lax.axis_index("head"), lax.axis_index("ctx")
    head_bits, ctx_bits = head_n.bit_length() - 1, ctx_n.bit_length() - 1
    bits = head_bits + ctx_bits
    me = ctx_i * head_n + head_i
    tok = queries.shape[0]
    heads = level_table.shape[2] * head_n
    width = queries.shape[1] // heads
    low = tok.bit_length() - 1
    stretches = tok // STRETCH

    table = lax.all_gather(level_table, "head", axis=2, tiled=True)
    mine = lax.dynamic_slice(selector, (head_i * stretches,), (stretches,))
    ids = jnp.arange(level_table.shape[0], dtype=jnp.int32)
    hot = (mine[:, None] == ids[None, :]).astype(F32)
    lev = jnp.arange(level_table.shape[1], dtype=jnp.int32).astype(F32)
    scaling = jnp.exp2(-0.5 * jnp.maximum(lev - 1.0, 0.0)) / math.sqrt(width)
    picked = jnp.sum(hot[:, :, None, None] * table[None], axis=1)
    lam = jnp.transpose(picked * scaling[None, :, None], (2, 0, 1))
    bit_ids = jnp.arange(bits, dtype=jnp.int32)
    upper = (me >> bit_ids & 1).astype(F32)
    lam_cross = lam[:, :, low + 1 : low + 1 + bits] * upper[None, None, :]

    row_spec = pl.BlockSpec((tok, GROUP * width), lambda h: (0, h))
    smem = pl.BlockSpec(memory_space=pltpu.SMEM)
    row_shape = jax.ShapeDtypeStruct(queries.shape, BF16)
    params = pltpu.CompilerParams(vmem_limit_bytes=VMEM_LIMIT)
    n_bytes = tok * heads * width * 2

    packet = pl.pallas_call(
        functools.partial(state_kernel, bits, low),
        grid=(heads // GROUP,),
        in_specs=[smem] + [row_spec] * 4,
        out_specs=pl.BlockSpec((bits + 1, GROUP, width, width), lambda h: (0, h, 0, 0)),
        out_shape=jax.ShapeDtypeStruct((bits + 1, heads, width, width), BF16),
        compiler_params=params,
        name="states",
    )(lam, queries, keys, values, out_grad)

    def dense(a, b, x, y, after, name):
        return pl.pallas_call(
            dense_kernel,
            grid=(heads // GROUP,),
            in_specs=[smem] + [row_spec] * 4 + [pl.BlockSpec(memory_space=pl.ANY)],
            out_specs=[row_spec] * 2 + [pl.BlockSpec((8, 128), lambda h: (0, 0))],
            out_shape=[row_shape] * 2 + [jax.ShapeDtypeStruct((8, 128), F32)],
            scratch_shapes=[pltpu.VMEM((GROUP, tok, tok), BF16)],
            compiler_params=params,
            cost_estimate=pl.CostEstimate(
                flops=8 * heads * tok * tok * width, bytes_accessed=6 * n_bytes, transcendentals=0
            ),
            name=name,
        )(lam, a, b, x, y, after)

    def swap(array, bit):
        if bit < head_bits:
            pairs = [(i, i ^ (1 << bit)) for i in range(head_n)]
            return lax.ppermute(array, "head", pairs)
        step = 1 << (bit - head_bits)
        return lax.ppermute(array, "ctx", [(i, i ^ step) for i in range(ctx_n)])

    def bit_of(bit):
        return (me >> bit & 1) == 1

    half = heads // 2
    core = head_i & 1
    got_full = swap(jnp.where(bit_of(0), packet[bits], packet[0]), 0)
    state0 = got_full
    back0 = jnp.where(bit_of(0), jnp.zeros_like(got_full), got_full)
    keep_i, send_i = core * half, (1 - core) * half
    sent = lax.dynamic_slice_in_dim(packet[:bits], send_i, half, axis=1)
    kept = lax.dynamic_slice_in_dim(packet[:bits], keep_i, half, axis=1)
    run = (kept.astype(F32) + swap(sent, 0).astype(F32)).astype(BF16)
    states = []
    back = jnp.zeros((half, width, width), F32)
    work = [
        (queries, keys, values, out_grad, "dense_out"),
        (out_grad, values, keys, queries, "dense_grad"),
    ]
    parts = []
    for bit in range(1, bits):
        last = bit == bits - 1
        sent = jnp.where(bit_of(bit), run[1], run[0]) if last else run
        got = swap(sent, bit).astype(F32)
        while work and (len(parts) < bit or last):
            *arrays, name = work.pop(0)
            first, second, token = dense(*arrays, sent, name)
            parts += [(first, second)]
            got = got + token[0, 0]
        if last:
            states.append(got.astype(BF16))
            back = back + jnp.where(bit_of(bit), 0.0, got)
        else:
            states.append(got[0].astype(BF16))
            back = back + jnp.where(bit_of(bit), 0.0, got[-1])
            run = (run[:-1].astype(F32) + got[:-1]).astype(BF16)
    (o_part, dv_part), (dq_part, dk_part) = parts
    ours = jnp.stack(states + [back.astype(BF16)], axis=0)
    theirs = swap(ours, 0)
    steps = half // GROUP
    pick = (jnp.arange(heads // GROUP, dtype=jnp.int32) // steps == core).astype(jnp.int32)

    mat_spec = pl.BlockSpec((GROUP, width, width), lambda h: (h, 0, 0))
    half_spec = pl.BlockSpec((bits, GROUP, width, width), lambda h: (0, h % steps, 0, 0))
    return pl.pallas_call(
        functools.partial(cross_kernel, bits),
        grid=(heads // GROUP,),
        in_specs=[smem] * 2 + [row_spec] * 8 + [mat_spec, half_spec, half_spec, mat_spec],
        out_specs=[row_spec] * 4,
        out_shape=[row_shape] * 4,
        compiler_params=params,
        name="cross",
    )(
        lam_cross, pick, queries, keys, values, out_grad,
        o_part, dq_part, dk_part, dv_part, state0, ours, theirs, back0,
    )


def solution(mesh):
    rows = P(("grp", "ctx", "head"), None)
    in_specs = (rows, rows, rows, rows, P(None, None, "head"), P(("grp", "ctx")))
    return jax.shard_map(
        shards, mesh=mesh, in_specs=in_specs, out_specs=(rows,) * 4, check_vma=False
    )
```

```python
import functools
import math

import jax
import jax.numpy as jnp
from jax import lax
from jax.experimental import pallas as pl
from jax.experimental.pallas import tpu as pltpu
from jax.sharding import PartitionSpec as P

F32 = jnp.float32
BF16 = jnp.bfloat16
STRETCH = 64
TILE = 128
NT = (((1,), (1,)), ((), ()))
TN = (((0,), (0,)), ((), ()))
NN = (((1,), (0,)), ((), ()))
VMEM_LIMIT = 62 * 1024 * 1024
GROUP = 2


def mm(a, b, dims):
    return lax.dot_general(a, b, dims, preferred_element_type=F32)


def state_kernel(bits, low, lam, q_all, k_all, v_all, g_all, out):
    tok = q_all.shape[0]
    width = q_all.shape[1] // GROUP
    for n in range(GROUP):
        head = pl.program_id(0) * GROUP + n
        lanes = slice(n * width, (n + 1) * width)
        q, k, v = q_all[:, lanes], k_all[:, lanes], v_all[:, lanes]
        grad = g_all[:, lanes].astype(F32)
        out[0, n] = mm(k, v, TN).astype(BF16)
        cols = []
        for j in range(bits):
            rows = [
                grad[c * STRETCH : (c + 1) * STRETCH] * lam[head, c, low + 1 + j]
                for c in range(tok // STRETCH)
            ]
            cols.append(jnp.concatenate(rows, axis=0).astype(BF16))
        outer = mm(q, jnp.concatenate(cols, axis=1), TN)
        for j in range(bits):
            out[bits - j, n] = outer[:, j * width : (j + 1) * width].astype(BF16)


def dense_kernel(first, lam, a, b, x, y, *refs):
    o1, o2, token, prob = refs[-4:]
    tok = a.shape[0]
    width = a.shape[1] // GROUP
    token[...] = jnp.zeros_like(token)
    ri = lax.broadcasted_iota(jnp.int32, (TILE, TILE), 0)
    ci = lax.broadcasted_iota(jnp.int32, (TILE, TILE), 1)
    xor = jnp.bitwise_xor(ri, ci)
    level = jnp.zeros((TILE, TILE), jnp.int32)
    tile_levels = TILE.bit_length() - 1
    for p in range(tile_levels):
        level = level + (xor >= (1 << p)).astype(jnp.int32)
    level = jnp.where(ci <= ri, level, -1)
    big = min(256, tok)
    for n in range(GROUP):
        head = (pl.program_id(0) + first) * GROUP + n
        lanes = slice(n * width, (n + 1) * width)
        for r0 in range(0, tok, big):
            cols = r0 + big
            scores = mm(a[r0 : r0 + big, lanes], b[:cols, lanes], NT)
            for r in range(r0 // TILE, (r0 + big) // TILE):
                for half in range(TILE // STRETCH):
                    row = r * TILE + half * STRETCH
                    c = row // STRETCH
                    for t in range(cols // TILE):
                        part = scores[row - r0 : row - r0 + STRETCH, t * TILE : (t + 1) * TILE]
                        if t < r:
                            part = part * lam[head, c, tile_levels + (r ^ t).bit_length()]
                        elif t == r:
                            lev = level[half * STRETCH : (half + 1) * STRETCH]
                            weight = jnp.zeros((STRETCH, TILE), F32)
                            for i in range(tile_levels + 1):
                                weight = jnp.where(lev == i, lam[head, c, i], weight)
                            part = part * weight
                        else:
                            part = jnp.zeros_like(part)
                        prob[n, row : row + STRETCH, t * TILE : (t + 1) * TILE] = part.astype(BF16)
            o1[r0 : r0 + big, lanes] = mm(
                prob[n, r0 : r0 + big, :cols], x[:cols, lanes], NN
            ).astype(BF16)
        for c0 in range(0, tok, big):
            o2[c0 : c0 + big, lanes] = mm(
                prob[n, c0:, c0 : c0 + big], y[c0:, lanes], TN
            ).astype(BF16)


def cross_kernel(
    bits, lam, pick, q, k, v, g, o_in, dq_in, dk_in, dv_in, x0, ours, theirs, o, dq, dk, dv
):
    tok = q.shape[0]
    width = q.shape[1] // GROUP
    own = pick[pl.program_id(0)] == 1
    lower = pick[pl.num_programs(0)] == 1
    for n in range(GROUP):
        head = pl.program_id(0) * GROUP + n
        lanes = slice(n * width, (n + 1) * width)
        rest = [jnp.where(own, ours[j, n], theirs[j, n]) for j in range(bits)]
        back = rest[bits - 1].astype(F32) + jnp.where(lower, x0[n].astype(F32), 0.0)
        back = back.astype(BF16)
        dk[:, lanes] = (dk_in[:, lanes].astype(F32) + mm(v[:, lanes], back, NT)).astype(BF16)
        dv[:, lanes] = (dv_in[:, lanes].astype(F32) + mm(k[:, lanes], back, NN)).astype(BF16)
        states = [x0[n]] + rest[: bits - 1]
        fwd = mm(q[:, lanes], jnp.concatenate(states, axis=1), NN)
        bwd = mm(g[:, lanes], jnp.concatenate(states, axis=0), NT)
        for c in range(tok // STRETCH):
            rows = slice(c * STRETCH, (c + 1) * STRETCH)
            o_sum = o_in[rows, lanes].astype(F32)
            q_sum = dq_in[rows, lanes].astype(F32)
            for j in range(bits):
                scale = lam[head, c, j]
                o_sum = o_sum + fwd[rows, j * width : (j + 1) * width] * scale
                q_sum = q_sum + bwd[rows, j * width : (j + 1) * width] * scale
            o[rows, lanes] = o_sum.astype(BF16)
            dq[rows, lanes] = q_sum.astype(BF16)


def shards(queries, keys, values, out_grad, level_table, selector):
    head_n, ctx_n = lax.axis_size("head"), lax.axis_size("ctx")
    head_i, ctx_i = lax.axis_index("head"), lax.axis_index("ctx")
    head_bits, ctx_bits = head_n.bit_length() - 1, ctx_n.bit_length() - 1
    bits = head_bits + ctx_bits
    me = ctx_i * head_n + head_i
    tok = queries.shape[0]
    heads = level_table.shape[2] * head_n
    width = queries.shape[1] // heads
    low = tok.bit_length() - 1
    stretches = tok // STRETCH

    table = lax.all_gather(level_table, "head", axis=2, tiled=True)
    mine = lax.dynamic_slice(selector, (head_i * stretches,), (stretches,))
    ids = jnp.arange(level_table.shape[0], dtype=jnp.int32)
    hot = (mine[:, None] == ids[None, :]).astype(F32)
    lev = jnp.arange(level_table.shape[1], dtype=jnp.int32).astype(F32)
    scaling = jnp.exp2(-0.5 * jnp.maximum(lev - 1.0, 0.0)) / math.sqrt(width)
    picked = jnp.sum(hot[:, :, None, None] * table[None], axis=1)
    lam = jnp.transpose(picked * scaling[None, :, None], (2, 0, 1))
    bit_ids = jnp.arange(bits, dtype=jnp.int32)
    upper = (me >> bit_ids & 1).astype(F32)
    lam_cross = lam[:, :, low + 1 : low + 1 + bits] * upper[None, None, :]

    row_spec = pl.BlockSpec((tok, GROUP * width), lambda h: (0, h))
    smem = pl.BlockSpec(memory_space=pltpu.SMEM)
    row_shape = jax.ShapeDtypeStruct(queries.shape, BF16)
    params = pltpu.CompilerParams(vmem_limit_bytes=VMEM_LIMIT)
    n_bytes = tok * heads * width * 2

    packet = pl.pallas_call(
        functools.partial(state_kernel, bits, low),
        grid=(heads // GROUP,),
        in_specs=[smem] + [row_spec] * 4,
        out_specs=pl.BlockSpec((bits + 1, GROUP, width, width), lambda h: (0, h, 0, 0)),
        out_shape=jax.ShapeDtypeStruct((bits + 1, heads, width, width), BF16),
        compiler_params=params,
        name="states",
    )(lam, queries, keys, values, out_grad)

    groups = heads // GROUP

    def dense(arrays, first, count, into, after, name):
        part_spec = pl.BlockSpec((tok, GROUP * width), lambda h: (0, h + first))
        anywhere = pl.BlockSpec(memory_space=pl.ANY)
        return pl.pallas_call(
            functools.partial(dense_kernel, first),
            grid=(count,),
            in_specs=[smem] + [part_spec] * 4 + [anywhere] * (len(into) + len(after)),
            out_specs=[part_spec] * 2 + [pl.BlockSpec((8, 128), lambda h: (0, 0))],
            out_shape=[row_shape] * 2 + [jax.ShapeDtypeStruct((8, 128), F32)],
            input_output_aliases={5 + i: i for i in range(len(into))},
            scratch_shapes=[pltpu.VMEM((GROUP, tok, tok), BF16)],
            compiler_params=params,
            cost_estimate=pl.CostEstimate(
                flops=8 * count * GROUP * tok * tok * width,
                bytes_accessed=6 * n_bytes * count // groups,
                transcendentals=0,
            ),
            name=name,
        )(lam, *arrays, *into, *after)

    def swap(array, bit):
        if bit < head_bits:
            pairs = [(i, i ^ (1 << bit)) for i in range(head_n)]
            return lax.ppermute(array, "head", pairs)
        step = 1 << (bit - head_bits)
        return lax.ppermute(array, "ctx", [(i, i ^ step) for i in range(ctx_n)])

    def bit_of(bit):
        return (me >> bit & 1) == 1

    half = heads // 2
    core = head_i & 1
    got_full = swap(jnp.where(bit_of(0), packet[bits], packet[0]), 0)
    state0 = got_full
    keep_i, send_i = core * half, (1 - core) * half
    sent = lax.dynamic_slice_in_dim(packet[:bits], send_i, half, axis=1)
    kept = lax.dynamic_slice_in_dim(packet[:bits], keep_i, half, axis=1)
    run = (kept.astype(F32) + swap(sent, 0).astype(F32)).astype(BF16)
    forward = (queries, keys, values, out_grad)
    backward = (out_grad, values, keys, queries)
    dense_parts = {}

    def dense_out(after):
        *dense_parts["out"], token = dense(forward, 0, groups, (), after, "dense_out")
        return token

    def dense_low(after):
        *dense_parts["grad"], token = dense(backward, 0, groups // 2, (), after, "dense_low")
        return token

    def dense_high(after):
        *dense_parts["grad"], token = dense(
            backward, groups // 2, groups - groups // 2, dense_parts["grad"], after, "dense_high"
        )
        return token

    work = [dense_out, dense_low, dense_high]

    def beside(sent, last):
        zero = 0.0
        while work:
            zero = zero + work.pop(0)([sent, state0] if last else [sent])[0, 0]
            if not last:
                break
        return zero

    quarter = half // 2
    side = head_i >> 1 & 1
    square = (width, width)
    whole = jnp.where(bit_of(1), run[-1], run[0])
    away = lax.dynamic_slice_in_dim(run[:-1], (1 - side) * quarter, quarter, axis=1)
    stay = lax.dynamic_slice_in_dim(run[:-1], side * quarter, quarter, axis=1)
    sent = jnp.concatenate([whole.reshape((2, quarter) + square), away], axis=0)
    got = swap(sent, 1)
    state1 = got[:2].reshape((half,) + square)
    run = (stay.astype(F32) + got[2:].astype(F32) + beside(sent, False)).astype(BF16)
    states = []
    back = jnp.zeros((quarter,) + square, F32)
    for bit in range(2, bits):
        last = bit == bits - 1
        sent = jnp.where(bit_of(bit), run[1], run[0]) if last else run
        got = swap(sent, bit)
        zero = beside(sent, last)
        if last:
            states.append((got.astype(F32) + zero).astype(BF16))
            back = back + jnp.where(bit_of(bit), 0.0, got.astype(F32))
        else:
            states.append(got[0])
            back = back + jnp.where(bit_of(bit), 0.0, got[-1].astype(F32))
            run = (run[:-1].astype(F32) + got[:-1].astype(F32) + zero).astype(BF16)
    near = jnp.stack(states + [back.astype(BF16)], axis=0)
    far = swap(near, 1)
    both = jnp.where(
        bit_of(1), jnp.concatenate([far, near], axis=1), jnp.concatenate([near, far], axis=1)
    )
    back1 = jnp.where(bit_of(1), 0.0, state1.astype(F32))
    total = (both[-1].astype(F32) + back1).astype(BF16)
    ours = jnp.concatenate([state1[None], both[:-1], total[None]], axis=0)
    theirs = swap(ours, 0)
    o_part, dv_part = dense_parts["out"]
    dq_part, dk_part = dense_parts["grad"]
    steps = half // GROUP
    pick = (jnp.arange(groups, dtype=jnp.int32) // steps == core).astype(jnp.int32)
    pick = jnp.concatenate([pick, (1 - core).astype(jnp.int32)[None]])

    mat_spec = pl.BlockSpec((GROUP, width, width), lambda h: (h, 0, 0))
    half_spec = pl.BlockSpec((bits, GROUP, width, width), lambda h: (0, h % steps, 0, 0))
    return pl.pallas_call(
        functools.partial(cross_kernel, bits),
        grid=(heads // GROUP,),
        in_specs=[smem] * 2 + [row_spec] * 8 + [mat_spec, half_spec, half_spec],
        out_specs=[row_spec] * 4,
        out_shape=[row_shape] * 4,
        compiler_params=params,
        name="cross",
    )(
        lam_cross, pick, queries, keys, values, out_grad,
        o_part, dq_part, dk_part, dv_part, state0, ours, theirs,
    )


def solution(mesh):
    rows = P(("grp", "ctx", "head"), None)
    in_specs = (rows, rows, rows, rows, P(None, None, "head"), P(("grp", "ctx")))
    return jax.shard_map(
        shards, mesh=mesh, in_specs=in_specs, out_specs=(rows,) * 4, check_vma=False
    )
```

```python
import functools
import math

import jax
import jax.numpy as jnp
from jax import lax
from jax.experimental import pallas as pl
from jax.experimental.pallas import tpu as pltpu
from jax.sharding import PartitionSpec as P

F32 = jnp.float32
BF16 = jnp.bfloat16
STRETCH = 64
TILE = 128
NT = (((1,), (1,)), ((), ()))
TN = (((0,), (0,)), ((), ()))
NN = (((1,), (0,)), ((), ()))
VMEM_LIMIT = 62 * 1024 * 1024
GROUP = 2


def mm(a, b, dims):
    return lax.dot_general(a, b, dims, preferred_element_type=F32)


def state_kernel(bits, low, lam, q_all, k_all, v_all, g_all, out):
    tok = q_all.shape[0]
    width = q_all.shape[1] // GROUP
    for n in range(GROUP):
        head = pl.program_id(0) * GROUP + n
        lanes = slice(n * width, (n + 1) * width)
        q, k, v = q_all[:, lanes], k_all[:, lanes], v_all[:, lanes]
        grad = g_all[:, lanes].astype(F32)
        out[0, n] = mm(k, v, TN).astype(BF16)
        cols = []
        for j in range(bits):
            rows = [
                grad[c * STRETCH : (c + 1) * STRETCH] * lam[head, c, low + 1 + j]
                for c in range(tok // STRETCH)
            ]
            cols.append(jnp.concatenate(rows, axis=0).astype(BF16))
        outer = mm(q, jnp.concatenate(cols, axis=1), TN)
        for j in range(bits):
            out[bits - j, n] = outer[:, j * width : (j + 1) * width].astype(BF16)


def dense_kernel(first, lam, a, b, x, y, *refs):
    o1, o2, token, prob = refs[-4:]
    tok = a.shape[0]
    width = a.shape[1] // GROUP
    token[...] = jnp.zeros_like(token)
    ri = lax.broadcasted_iota(jnp.int32, (TILE, TILE), 0)
    ci = lax.broadcasted_iota(jnp.int32, (TILE, TILE), 1)
    xor = jnp.bitwise_xor(ri, ci)
    level = jnp.zeros((TILE, TILE), jnp.int32)
    tile_levels = TILE.bit_length() - 1
    for p in range(tile_levels):
        level = level + (xor >= (1 << p)).astype(jnp.int32)
    level = jnp.where(ci <= ri, level, -1)
    big = min(256, tok)
    for n in range(GROUP):
        head = (pl.program_id(0) + first) * GROUP + n
        lanes = slice(n * width, (n + 1) * width)
        for r0 in range(0, tok, big):
            cols = r0 + big
            scores = mm(a[r0 : r0 + big, lanes], b[:cols, lanes], NT)
            for r in range(r0 // TILE, (r0 + big) // TILE):
                for half in range(TILE // STRETCH):
                    row = r * TILE + half * STRETCH
                    c = row // STRETCH
                    for t in range(cols // TILE):
                        part = scores[row - r0 : row - r0 + STRETCH, t * TILE : (t + 1) * TILE]
                        if t < r:
                            part = part * lam[head, c, tile_levels + (r ^ t).bit_length()]
                        elif t == r:
                            lev = level[half * STRETCH : (half + 1) * STRETCH]
                            weight = jnp.zeros((STRETCH, TILE), F32)
                            for i in range(tile_levels + 1):
                                weight = jnp.where(lev == i, lam[head, c, i], weight)
                            part = part * weight
                        else:
                            part = jnp.zeros_like(part)
                        prob[n, row : row + STRETCH, t * TILE : (t + 1) * TILE] = part.astype(BF16)
            o1[r0 : r0 + big, lanes] = mm(
                prob[n, r0 : r0 + big, :cols], x[:cols, lanes], NN
            ).astype(BF16)
        for c0 in range(0, tok, big):
            o2[c0 : c0 + big, lanes] = mm(
                prob[n, c0:, c0 : c0 + big], y[c0:, lanes], TN
            ).astype(BF16)


def cross_kernel(
    bits, lam, pick, q, k, v, g, o_in, dq_in, dk_in, dv_in, x0, ours, theirs, o, dq, dk, dv
):
    tok = q.shape[0]
    width = q.shape[1] // GROUP
    own = pick[pl.program_id(0)] == 1
    lower = pick[pl.num_programs(0)] == 1
    for n in range(GROUP):
        head = pl.program_id(0) * GROUP + n
        lanes = slice(n * width, (n + 1) * width)
        rest = [jnp.where(own, ours[j, n], theirs[j, n]) for j in range(bits)]
        back = rest[bits - 1].astype(F32) + jnp.where(lower, x0[n].astype(F32), 0.0)
        back = back.astype(BF16)
        dk[:, lanes] = (dk_in[:, lanes].astype(F32) + mm(v[:, lanes], back, NT)).astype(BF16)
        dv[:, lanes] = (dv_in[:, lanes].astype(F32) + mm(k[:, lanes], back, NN)).astype(BF16)
        states = [x0[n]] + rest[: bits - 1]
        sides = ((q, states, 0, NN, o_in, o), (g, states, 1, NT, dq_in, dq))
        for rows_in, mats, axis, dims, part, result in sides:
            full = rows_in[:, lanes].astype(F32)
            scaled = []
            for j in range(bits):
                pieces = [
                    full[c * STRETCH : (c + 1) * STRETCH] * lam[head, c, j]
                    for c in range(tok // STRETCH)
                ]
                scaled.append(jnp.concatenate(pieces, axis=0).astype(BF16))
            total = mm(jnp.concatenate(scaled, axis=1), jnp.concatenate(mats, axis=axis), dims)
            result[:, lanes] = (part[:, lanes].astype(F32) + total).astype(BF16)


def shards(queries, keys, values, out_grad, level_table, selector):
    head_n, ctx_n = lax.axis_size("head"), lax.axis_size("ctx")
    head_i, ctx_i = lax.axis_index("head"), lax.axis_index("ctx")
    head_bits, ctx_bits = head_n.bit_length() - 1, ctx_n.bit_length() - 1
    bits = head_bits + ctx_bits
    me = ctx_i * head_n + head_i
    tok = queries.shape[0]
    heads = level_table.shape[2] * head_n
    width = queries.shape[1] // heads
    low = tok.bit_length() - 1
    stretches = tok // STRETCH

    table = lax.all_gather(level_table, "head", axis=2, tiled=True)
    mine = lax.dynamic_slice(selector, (head_i * stretches,), (stretches,))
    ids = jnp.arange(level_table.shape[0], dtype=jnp.int32)
    hot = (mine[:, None] == ids[None, :]).astype(F32)
    lev = jnp.arange(level_table.shape[1], dtype=jnp.int32).astype(F32)
    scaling = jnp.exp2(-0.5 * jnp.maximum(lev - 1.0, 0.0)) / math.sqrt(width)
    picked = jnp.sum(hot[:, :, None, None] * table[None], axis=1)
    lam = jnp.transpose(picked * scaling[None, :, None], (2, 0, 1))
    bit_ids = jnp.arange(bits, dtype=jnp.int32)
    upper = (me >> bit_ids & 1).astype(F32)
    lam_cross = lam[:, :, low + 1 : low + 1 + bits] * upper[None, None, :]

    row_spec = pl.BlockSpec((tok, GROUP * width), lambda h: (0, h))
    smem = pl.BlockSpec(memory_space=pltpu.SMEM)
    row_shape = jax.ShapeDtypeStruct(queries.shape, BF16)
    params = pltpu.CompilerParams(vmem_limit_bytes=VMEM_LIMIT)
    n_bytes = tok * heads * width * 2

    packet = pl.pallas_call(
        functools.partial(state_kernel, bits, low),
        grid=(heads // GROUP,),
        in_specs=[smem] + [row_spec] * 4,
        out_specs=pl.BlockSpec((bits + 1, GROUP, width, width), lambda h: (0, h, 0, 0)),
        out_shape=jax.ShapeDtypeStruct((bits + 1, heads, width, width), BF16),
        compiler_params=params,
        name="states",
    )(lam, queries, keys, values, out_grad)

    groups = heads // GROUP

    def dense(arrays, first, count, into, after, name):
        part_spec = pl.BlockSpec((tok, GROUP * width), lambda h: (0, h + first))
        anywhere = pl.BlockSpec(memory_space=pl.ANY)
        return pl.pallas_call(
            functools.partial(dense_kernel, first),
            grid=(count,),
            in_specs=[smem] + [part_spec] * 4 + [anywhere] * (len(into) + len(after)),
            out_specs=[part_spec] * 2 + [pl.BlockSpec((8, 128), lambda h: (0, 0))],
            out_shape=[row_shape] * 2 + [jax.ShapeDtypeStruct((8, 128), F32)],
            input_output_aliases={5 + i: i for i in range(len(into))},
            scratch_shapes=[pltpu.VMEM((GROUP, tok, tok), BF16)],
            compiler_params=params,
            cost_estimate=pl.CostEstimate(
                flops=8 * count * GROUP * tok * tok * width,
                bytes_accessed=6 * n_bytes * count // groups,
                transcendentals=0,
            ),
            name=name,
        )(lam, *arrays, *into, *after)

    def swap(array, bit):
        if bit < head_bits:
            pairs = [(i, i ^ (1 << bit)) for i in range(head_n)]
            return lax.ppermute(array, "head", pairs)
        step = 1 << (bit - head_bits)
        return lax.ppermute(array, "ctx", [(i, i ^ step) for i in range(ctx_n)])

    def bit_of(bit):
        return (me >> bit & 1) == 1

    half = heads // 2
    core = head_i & 1
    got_full = swap(jnp.where(bit_of(0), packet[bits], packet[0]), 0)
    state0 = got_full
    keep_i, send_i = core * half, (1 - core) * half
    sent = lax.dynamic_slice_in_dim(packet[:bits], send_i, half, axis=1)
    kept = lax.dynamic_slice_in_dim(packet[:bits], keep_i, half, axis=1)
    run = (kept.astype(F32) + swap(sent, 0).astype(F32)).astype(BF16)
    forward = (queries, keys, values, out_grad)
    backward = (out_grad, values, keys, queries)
    dense_parts = {}

    def dense_out(after):
        *dense_parts["out"], token = dense(forward, 0, groups, (), after, "dense_out")
        return token

    def dense_low(after):
        *dense_parts["grad"], token = dense(backward, 0, groups // 2, (), after, "dense_low")
        return token

    def dense_high(after):
        *dense_parts["grad"], token = dense(
            backward, groups // 2, groups - groups // 2, dense_parts["grad"], after, "dense_high"
        )
        return token

    work = [dense_out, dense_low, dense_high]

    def beside(sent):
        return work.pop(0)(sent)[0, 0]

    quarter = half // 2
    side = head_i >> 1 & 1
    square = (width, width)
    whole = jnp.where(bit_of(1), run[-1], run[0])
    away = lax.dynamic_slice_in_dim(run[:-1], (1 - side) * quarter, quarter, axis=1)
    stay = lax.dynamic_slice_in_dim(run[:-1], side * quarter, quarter, axis=1)
    sent = jnp.concatenate([whole.reshape((2, quarter) + square), away], axis=0)
    got = swap(sent, 1)
    state1 = got[:2].reshape((half,) + square)
    run = (stay.astype(F32) + got[2:].astype(F32) + beside([sent])).astype(BF16)
    states = []
    back = jnp.zeros((quarter,) + square, F32)
    for bit in range(2, bits):
        last = bit == bits - 1
        sent = jnp.where(bit_of(bit), run[1], run[0]) if last else run
        got = swap(sent, bit)
        zero = beside([sent]) if bit == 2 else 0.0
        if last:
            states.append((got.astype(F32) + zero).astype(BF16))
            back = back + jnp.where(bit_of(bit), 0.0, got.astype(F32))
        else:
            states.append(got[0])
            back = back + jnp.where(bit_of(bit), 0.0, got[-1].astype(F32))
            run = (run[:-1].astype(F32) + got[:-1].astype(F32) + zero).astype(BF16)
    near = jnp.stack(states + [back.astype(BF16)], axis=0)
    far = (swap(near, 1).astype(F32) + beside([near, state0])).astype(BF16)
    both = jnp.where(
        bit_of(1), jnp.concatenate([far, near], axis=1), jnp.concatenate([near, far], axis=1)
    )
    back1 = jnp.where(bit_of(1), 0.0, state1.astype(F32))
    total = (both[-1].astype(F32) + back1).astype(BF16)
    ours = jnp.concatenate([state1[None], both[:-1], total[None]], axis=0)
    theirs = swap(ours, 0)
    o_part, dv_part = dense_parts["out"]
    dq_part, dk_part = dense_parts["grad"]
    steps = half // GROUP
    pick = (jnp.arange(groups, dtype=jnp.int32) // steps == core).astype(jnp.int32)
    pick = jnp.concatenate([pick, (1 - core).astype(jnp.int32)[None]])

    mat_spec = pl.BlockSpec((GROUP, width, width), lambda h: (h, 0, 0))
    half_spec = pl.BlockSpec((bits, GROUP, width, width), lambda h: (0, h % steps, 0, 0))
    return pl.pallas_call(
        functools.partial(cross_kernel, bits),
        grid=(heads // GROUP,),
        in_specs=[smem] * 2 + [row_spec] * 8 + [mat_spec, half_spec, half_spec],
        out_specs=[row_spec] * 4,
        out_shape=[row_shape] * 4,
        compiler_params=params,
        name="cross",
    )(
        lam_cross, pick, queries, keys, values, out_grad,
        o_part, dq_part, dk_part, dv_part, state0, ours, theirs,
    )


def solution(mesh):
    rows = P(("grp", "ctx", "head"), None)
    in_specs = (rows, rows, rows, rows, P(None, None, "head"), P(("grp", "ctx")))
    return jax.shard_map(
        shards, mesh=mesh, in_specs=in_specs, out_specs=(rows,) * 4, check_vma=False
    )
```

```python
import functools
import math

import jax
import jax.numpy as jnp
from jax import lax
from jax.experimental import pallas as pl
from jax.experimental.pallas import tpu as pltpu
from jax.sharding import PartitionSpec as P

F32 = jnp.float32
BF16 = jnp.bfloat16
STRETCH = 64
TILE = 128
NT = (((1,), (1,)), ((), ()))
TN = (((0,), (0,)), ((), ()))
NN = (((1,), (0,)), ((), ()))
VMEM_LIMIT = 62 * 1024 * 1024
GROUP = 2
WIDE = 4


def mm(a, b, dims):
    return lax.dot_general(a, b, dims, preferred_element_type=F32)


def state_kernel(bits, low, lam, q_all, k_all, v_all, g_all, out):
    tok = q_all.shape[0]
    width = q_all.shape[1] // GROUP
    for n in range(GROUP):
        head = pl.program_id(0) * GROUP + n
        lanes = slice(n * width, (n + 1) * width)
        q, k, v = q_all[:, lanes], k_all[:, lanes], v_all[:, lanes]
        grad = g_all[:, lanes].astype(F32)
        out[0, n] = mm(k, v, TN).astype(BF16)
        cols = []
        for j in range(bits):
            rows = [
                grad[c * STRETCH : (c + 1) * STRETCH] * lam[head, c, low + 1 + j]
                for c in range(tok // STRETCH)
            ]
            cols.append(jnp.concatenate(rows, axis=0).astype(BF16))
        outer = mm(q, jnp.concatenate(cols, axis=1), TN)
        for j in range(bits):
            out[bits - j, n] = outer[:, j * width : (j + 1) * width].astype(BF16)


def dense_kernel(first, lam, a, b, x, y, *refs):
    o1, o2, token, prob = refs[-4:]
    tok = a.shape[0]
    width = a.shape[1] // GROUP
    token[...] = jnp.zeros_like(token)
    ri = lax.broadcasted_iota(jnp.int32, (TILE, TILE), 0)
    ci = lax.broadcasted_iota(jnp.int32, (TILE, TILE), 1)
    xor = jnp.bitwise_xor(ri, ci)
    level = jnp.zeros((TILE, TILE), jnp.int32)
    tile_levels = TILE.bit_length() - 1
    for p in range(tile_levels):
        level = level + (xor >= (1 << p)).astype(jnp.int32)
    level = jnp.where(ci <= ri, level, -1)
    big = min(256, tok)
    for n in range(GROUP):
        head = (pl.program_id(0) + first) * GROUP + n
        lanes = slice(n * width, (n + 1) * width)
        for r0 in range(0, tok, big):
            cols = r0 + big
            scores = mm(a[r0 : r0 + big, lanes], b[:cols, lanes], NT)
            for r in range(r0 // TILE, (r0 + big) // TILE):
                for half in range(TILE // STRETCH):
                    row = r * TILE + half * STRETCH
                    c = row // STRETCH
                    for t in range(cols // TILE):
                        part = scores[row - r0 : row - r0 + STRETCH, t * TILE : (t + 1) * TILE]
                        if t < r:
                            part = part * lam[head, c, tile_levels + (r ^ t).bit_length()]
                        elif t == r:
                            lev = level[half * STRETCH : (half + 1) * STRETCH]
                            weight = jnp.zeros((STRETCH, TILE), F32)
                            for i in range(tile_levels + 1):
                                weight = jnp.where(lev == i, lam[head, c, i], weight)
                            part = part * weight
                        else:
                            part = jnp.zeros_like(part)
                        prob[n, row : row + STRETCH, t * TILE : (t + 1) * TILE] = part.astype(BF16)
            o1[r0 : r0 + big, lanes] = mm(
                prob[n, r0 : r0 + big, :cols], x[:cols, lanes], NN
            ).astype(BF16)
        for c0 in range(0, tok, big):
            o2[c0 : c0 + big, lanes] = mm(
                prob[n, c0:, c0 : c0 + big], y[c0:, lanes], TN
            ).astype(BF16)


def cross_kernel(
    bits, lam, pick, q, k, v, g, o_in, dq_in, dk_in, dv_in, x0, ours, theirs, o, dq, dk, dv
):
    tok = q.shape[0]
    width = q.shape[1] // WIDE
    own = pick[pl.program_id(0)] == 1
    lower = pick[pl.num_programs(0)] == 1
    for n in range(WIDE):
        head = pl.program_id(0) * WIDE + n
        lanes = slice(n * width, (n + 1) * width)
        rest = [jnp.where(own, ours[j, n], theirs[j, n]) for j in range(bits)]
        back = rest[bits - 1].astype(F32) + jnp.where(lower, x0[n].astype(F32), 0.0)
        back = back.astype(BF16)
        dk[:, lanes] = (dk_in[:, lanes].astype(F32) + mm(v[:, lanes], back, NT)).astype(BF16)
        dv[:, lanes] = (dv_in[:, lanes].astype(F32) + mm(k[:, lanes], back, NN)).astype(BF16)
        states = [x0[n]] + rest[: bits - 1]
        sides = ((q, states, 0, NN, o_in, o), (g, states, 1, NT, dq_in, dq))
        for rows_in, mats, axis, dims, part, result in sides:
            full = rows_in[:, lanes].astype(F32)
            scaled = []
            for j in range(bits):
                pieces = [
                    full[c * STRETCH : (c + 1) * STRETCH] * lam[head, c, j]
                    for c in range(tok // STRETCH)
                ]
                scaled.append(jnp.concatenate(pieces, axis=0).astype(BF16))
            total = mm(jnp.concatenate(scaled, axis=1), jnp.concatenate(mats, axis=axis), dims)
            result[:, lanes] = (part[:, lanes].astype(F32) + total).astype(BF16)


def shards(queries, keys, values, out_grad, level_table, selector):
    head_n, ctx_n = lax.axis_size("head"), lax.axis_size("ctx")
    head_i, ctx_i = lax.axis_index("head"), lax.axis_index("ctx")
    head_bits, ctx_bits = head_n.bit_length() - 1, ctx_n.bit_length() - 1
    bits = head_bits + ctx_bits
    me = ctx_i * head_n + head_i
    tok = queries.shape[0]
    heads = level_table.shape[2] * head_n
    width = queries.shape[1] // heads
    low = tok.bit_length() - 1
    stretches = tok // STRETCH

    table = lax.all_gather(level_table, "head", axis=2, tiled=True)
    mine = lax.dynamic_slice(selector, (head_i * stretches,), (stretches,))
    ids = jnp.arange(level_table.shape[0], dtype=jnp.int32)
    hot = (mine[:, None] == ids[None, :]).astype(F32)
    lev = jnp.arange(level_table.shape[1], dtype=jnp.int32).astype(F32)
    scaling = jnp.exp2(-0.5 * jnp.maximum(lev - 1.0, 0.0)) / math.sqrt(width)
    picked = jnp.sum(hot[:, :, None, None] * table[None], axis=1)
    lam = jnp.transpose(picked * scaling[None, :, None], (2, 0, 1))
    bit_ids = jnp.arange(bits, dtype=jnp.int32)
    upper = (me >> bit_ids & 1).astype(F32)
    lam_cross = lam[:, :, low + 1 : low + 1 + bits] * upper[None, None, :]

    row_spec = pl.BlockSpec((tok, GROUP * width), lambda h: (0, h))
    smem = pl.BlockSpec(memory_space=pltpu.SMEM)
    row_shape = jax.ShapeDtypeStruct(queries.shape, BF16)
    params = pltpu.CompilerParams(vmem_limit_bytes=VMEM_LIMIT)
    n_bytes = tok * heads * width * 2

    packet = pl.pallas_call(
        functools.partial(state_kernel, bits, low),
        grid=(heads // GROUP,),
        in_specs=[smem] + [row_spec] * 4,
        out_specs=pl.BlockSpec((bits + 1, GROUP, width, width), lambda h: (0, h, 0, 0)),
        out_shape=jax.ShapeDtypeStruct((bits + 1, heads, width, width), BF16),
        compiler_params=params,
        name="states",
    )(lam, queries, keys, values, out_grad)

    groups = heads // GROUP

    def dense(arrays, first, count, into, after, name):
        part_spec = pl.BlockSpec((tok, GROUP * width), lambda h: (0, h + first))
        anywhere = pl.BlockSpec(memory_space=pl.ANY)
        return pl.pallas_call(
            functools.partial(dense_kernel, first),
            grid=(count,),
            in_specs=[smem] + [part_spec] * 4 + [anywhere] * (len(into) + len(after)),
            out_specs=[part_spec] * 2 + [pl.BlockSpec((8, 128), lambda h: (0, 0))],
            out_shape=[row_shape] * 2 + [jax.ShapeDtypeStruct((8, 128), F32)],
            input_output_aliases={5 + i: i for i in range(len(into))},
            scratch_shapes=[pltpu.VMEM((GROUP, tok, tok), BF16)],
            compiler_params=params,
            cost_estimate=pl.CostEstimate(
                flops=8 * count * GROUP * tok * tok * width,
                bytes_accessed=6 * n_bytes * count // groups,
                transcendentals=0,
            ),
            name=name,
        )(lam, *arrays, *into, *after)

    def swap(array, bit):
        if bit < head_bits:
            pairs = [(i, i ^ (1 << bit)) for i in range(head_n)]
            return lax.ppermute(array, "head", pairs)
        step = 1 << (bit - head_bits)
        return lax.ppermute(array, "ctx", [(i, i ^ step) for i in range(ctx_n)])

    def bit_of(bit):
        return (me >> bit & 1) == 1

    half = heads // 2
    core = head_i & 1
    got_full = swap(jnp.where(bit_of(0), packet[bits], packet[0]), 0)
    state0 = got_full
    keep_i, send_i = core * half, (1 - core) * half
    sent = lax.dynamic_slice_in_dim(packet[:bits], send_i, half, axis=1)
    kept = lax.dynamic_slice_in_dim(packet[:bits], keep_i, half, axis=1)
    run = (kept.astype(F32) + swap(sent, 0).astype(F32)).astype(BF16)
    forward = (queries, keys, values, out_grad)
    backward = (out_grad, values, keys, queries)
    dense_parts = {}

    def dense_out(after):
        *dense_parts["out"], token = dense(forward, 0, groups, (), after, "dense_out")
        return token

    def dense_low(after):
        *dense_parts["grad"], token = dense(backward, 0, groups // 2, (), after, "dense_low")
        return token

    def dense_high(after):
        *dense_parts["grad"], token = dense(
            backward, groups // 2, groups - groups // 2, dense_parts["grad"], after, "dense_high"
        )
        return token

    work = [dense_out, dense_low, dense_high]

    def beside(sent):
        return work.pop(0)(sent)[0, 0]

    quarter = half // 2
    side = head_i >> 1 & 1
    square = (width, width)
    whole = jnp.where(bit_of(1), run[-1], run[0])
    away = lax.dynamic_slice_in_dim(run[:-1], (1 - side) * quarter, quarter, axis=1)
    stay = lax.dynamic_slice_in_dim(run[:-1], side * quarter, quarter, axis=1)
    sent = jnp.concatenate([whole.reshape((2, quarter) + square), away], axis=0)
    got = swap(sent, 1)
    state1 = got[:2].reshape((half,) + square)
    run = (stay.astype(F32) + got[2:].astype(F32) + beside([sent])).astype(BF16)
    states = []
    back = jnp.zeros((quarter,) + square, F32)
    for bit in range(2, bits):
        last = bit == bits - 1
        sent = jnp.where(bit_of(bit), run[1], run[0]) if last else run
        got = swap(sent, bit)
        zero = beside([sent]) if bit == 2 else 0.0
        if last:
            states.append((got.astype(F32) + zero).astype(BF16))
            back = back + jnp.where(bit_of(bit), 0.0, got.astype(F32))
        else:
            states.append(got[0])
            back = back + jnp.where(bit_of(bit), 0.0, got[-1].astype(F32))
            run = (run[:-1].astype(F32) + got[:-1].astype(F32) + zero).astype(BF16)
    near = jnp.stack(states + [back.astype(BF16)], axis=0)
    far = (swap(near, 1).astype(F32) + beside([near, state0])).astype(BF16)
    both = jnp.where(
        bit_of(1), jnp.concatenate([far, near], axis=1), jnp.concatenate([near, far], axis=1)
    )
    back1 = jnp.where(bit_of(1), 0.0, state1.astype(F32))
    total = (both[-1].astype(F32) + back1).astype(BF16)
    ours = jnp.concatenate([state1[None], both[:-1], total[None]], axis=0)
    theirs = swap(ours, 0)
    o_part, dv_part = dense_parts["out"]
    dq_part, dk_part = dense_parts["grad"]
    steps = half // WIDE
    pick = (jnp.arange(heads // WIDE, dtype=jnp.int32) // steps == core).astype(jnp.int32)
    pick = jnp.concatenate([pick, (1 - core).astype(jnp.int32)[None]])

    wide_spec = pl.BlockSpec((tok, WIDE * width), lambda h: (0, h))
    mat_spec = pl.BlockSpec((WIDE, width, width), lambda h: (h, 0, 0))
    half_spec = pl.BlockSpec((bits, WIDE, width, width), lambda h: (0, h % steps, 0, 0))
    return pl.pallas_call(
        functools.partial(cross_kernel, bits),
        grid=(heads // WIDE,),
        in_specs=[smem] * 2 + [wide_spec] * 8 + [mat_spec, half_spec, half_spec],
        out_specs=[wide_spec] * 4,
        out_shape=[row_shape] * 4,
        compiler_params=params,
        name="cross",
    )(
        lam_cross, pick, queries, keys, values, out_grad,
        o_part, dq_part, dk_part, dv_part, state0, ours, theirs,
    )


def solution(mesh):
    rows = P(("grp", "ctx", "head"), None)
    in_specs = (rows, rows, rows, rows, P(None, None, "head"), P(("grp", "ctx")))
    return jax.shard_map(
        shards, mesh=mesh, in_specs=in_specs, out_specs=(rows,) * 4, check_vma=False
    )
```
